512 devices in a mesh: seq: 64 (over z, x_hi, core), grp: 8 (over x_lo, y).
Axes of the slice: x: 4 (x_hi: 2, x_lo: 2; x = x_hi * 2 + x_lo), y: 4, z: 16, core: 2. Of those that a mesh axis runs over, the one named last changes fastest.
Arguments:
- inputs: bfloat16 [65536, 2048], P('seq', 'grp'), may hold values from -6 to 6
- out_grad: bfloat16 [65536, 2048], P('seq', 'grp'), may hold values from -6 to 6
- filt: bfloat16 [128, 2048], P('grp'), may hold values from -0.125 to 0.125
- band: int32 [128, 16], P('grp'), may hold values from 0 to 1, as said below
Outputs:
- input_grad: bfloat16 [65536, 2048], P(('seq', 'grp'))
- filter_grad: float32 [128, 2048], P('grp', 'seq')
The draws below stay inside these ranges and needn't reach their ends.
Inputs may be any that keep to these rules, and one draw needn't show every extreme that they name: Each row of band is a truncation: ones at offsets 0 .. L - 1 and zeros after, with 1 <= L <= 16; some group keeps all 16 offsets.
All inputs are finite; a program needn't handle non-finite values.
Results may differ from the reference program's by a relative error of at most 0.001.
Values may be sent and summed in bfloat16 or wider, within the bound.
No kernel may reach another device: no remote copies, remote signals or barrier semaphores. Data moves between devices by JAX's collectives and lax.ppermute only.
A program may use at most 64 MiB of HBM per device.

```python
import math
import jax
import jax.numpy as jnp
from jax import lax

GROUPS = 128
CPG = 16
BLK = 128
NOFF = 16
WIDTH = 2048
TOKENS = 65536
FLEN = 2048
N_GRP = 8


def draw_band(key, part):
    per_block = GROUPS // N_GRP
    block_level = jax.random.randint(jax.random.fold_in(key, 11), (N_GRP,), 1, NOFF + 1)
    longest = jax.random.randint(jax.random.fold_in(key, 13), (), 0, N_GRP)
    block_level = jnp.where(jnp.arange(N_GRP, dtype=jnp.int32) == longest, NOFF, block_level)
    group_level = jnp.repeat(block_level, per_block)
    fraction = jax.random.randint(jax.random.fold_in(key, 12), (GROUPS,), 0, 1 << 20)
    level = 1 + fraction * group_level // (1 << 20)
    first = jnp.arange(GROUPS, dtype=jnp.int32) % per_block == 0
    level = jnp.where(first, group_level, level)
    offsets = jnp.arange(NOFF, dtype=jnp.int32)
    return (offsets[None, :] < level[:, None]).astype(jnp.int32)


def levels(key, dims, cuts, low, largest):
    gain, own = 1.0, jax.random.fold_in(key, 6)
    for axis_at, blocks in cuts:
        steps = jnp.exp(jax.random.uniform(jax.random.fold_in(own, axis_at), (blocks,), jnp.float32, low / len(cuts), largest / len(cuts)))
        gain = gain * jnp.repeat(steps, dims[axis_at] // blocks).reshape([-1 if axis == axis_at else 1 for axis in range(len(dims))])
    return gain


def normal_values(own_key, extent, scale, reach, cuts=(), kind=jnp.bfloat16):
    array = scale * jax.random.normal(own_key, extent, jnp.float32)
    if cuts:
        array = array * levels(own_key, extent, cuts, -0.22, 0.18)
    return jnp.clip(array, -reach, reach).astype(kind)


def setup_inputs(seed: int = 0) -> dict:
    streams_of = jax.random.split(jax.random.key(seed), 5)
    inputs = normal_values(streams_of[0], (TOKENS, WIDTH), 1.0, 6.0, ((0, 64), (1, 8)))
    out_grad = normal_values(streams_of[1], (TOKENS, WIDTH), 1.0, 6.0, ((0, 64), (1, 8)))
    filt = normal_values(streams_of[2], (GROUPS, FLEN), FLEN ** -0.5, 0.125, ((0, 8),))
    band = draw_band(jax.random.fold_in(streams_of[4], 71), 0)
    return {"inputs": inputs, "out_grad": out_grad, "filt": filt, "band": band}


def build_tile(filt_pad, keep, offset, width_blk):
    window = lax.dynamic_slice_in_dim(filt_pad, offset * width_blk, 2 * width_blk, 1)
    groups_here = window.shape[0]
    turned = jnp.roll(window[:, ::-1], -(width_blk - 1), axis=1)
    repeated = jnp.tile(turned, (1, width_blk))[:, :width_blk * (2 * width_blk - 1)]
    tile = repeated.reshape(groups_here, width_blk, 2 * width_blk - 1)[:, :, :width_blk]
    return jnp.where((keep > 0)[:, None, None], tile, jnp.zeros_like(tile))

def flip_pad(blocks):
    return jnp.concatenate([blocks[:, ::-1], jnp.zeros_like(blocks)], axis=1)

def diagonal_sums(product):
    groups_here = product.shape[0]
    width_blk = product.shape[1]
    flat = product.reshape(groups_here, 2 * width_blk * width_blk)[:, :width_blk * (2 * width_blk - 1)]
    return lax.optimization_barrier(jnp.sum(flat.reshape(groups_here, width_blk, 2 * width_blk - 1), axis=1))

def reference(inputs, out_grad, filt, band):
    total_rows, width = inputs.shape
    blocks_all = total_rows // BLK
    groups_all = width // CPG
    in_blocks = inputs.reshape(blocks_all, BLK, groups_all, CPG)
    grad_blocks = out_grad.reshape(blocks_all, BLK, groups_all, CPG)
    zero_blocks = jnp.zeros((NOFF, BLK, groups_all, CPG), jnp.bfloat16)
    grad_ext = jnp.concatenate([grad_blocks, zero_blocks], axis=0)
    in_ext = jnp.concatenate([zero_blocks, in_blocks], axis=0)
    filt_pad = jnp.concatenate([jnp.zeros((groups_all, BLK), jnp.bfloat16), filt], axis=1)

    def one_offset(carry, offset):
        dx_acc, dh_acc = carry
        keep = lax.dynamic_index_in_dim(band, offset, 1, keepdims=False)
        tile = build_tile(filt_pad, keep, offset, BLK)
        later = lax.dynamic_slice_in_dim(grad_ext, offset, blocks_all, 0)
        dx_acc = dx_acc + jnp.einsum('gab,jagc->jbgc', tile.astype(jnp.float32), later.astype(jnp.float32), precision=lax.Precision.HIGHEST)
        earlier = lax.dynamic_slice_in_dim(in_ext, NOFF - offset, blocks_all, 0)
        product = jnp.einsum('jagc,jbgc->gab', grad_blocks.astype(jnp.float32), flip_pad(earlier).astype(jnp.float32), precision=lax.Precision.HIGHEST)
        sums = diagonal_sums(product) * (keep > 0).astype(jnp.float32)[:, None]
        start = offset * BLK + 1
        current = lax.dynamic_slice_in_dim(dh_acc, start, 2 * BLK - 1, 1)
        dh_acc = lax.dynamic_update_slice_in_dim(dh_acc, current + sums, start, 1)
        return ((dx_acc, dh_acc), None)
    init = (jnp.zeros((blocks_all, BLK, groups_all, CPG), jnp.float32), jnp.zeros((groups_all, NOFF * BLK + BLK), jnp.float32))
    (dx_acc, dh_acc), _ = lax.scan(one_offset, init, jnp.arange(NOFF, dtype=jnp.int32))
    scale = 1.0 / math.sqrt(total_rows * CPG)
    input_grad = dx_acc.reshape(total_rows, width).astype(jnp.bfloat16)
    filter_grad = dh_acc[:, BLK:] * scale
    return (input_grad, filter_grad)
```

```python
import functools
import math

import jax
import jax.numpy as jnp
from jax import lax
from jax.experimental import pallas as pl
from jax.experimental.pallas import tpu as pltpu
from jax.sharding import Mesh
from jax.sharding import PartitionSpec as P

CPG = 16
BLK = 128
NOFF = 16
LANES = 128
QUART = 32
BF16 = jnp.bfloat16
F32 = jnp.float32
VMEM = pl.BlockSpec(memory_space=pltpu.VMEM)
SMEM = pl.BlockSpec(memory_space=pltpu.SMEM)
PARAMS = pltpu.CompilerParams(vmem_limit_bytes=48 << 20)


def aligned(start, size):
    return pl.ds(pl.multiple_of(start, size), size)


def tiles_kernel(level, turned_filt, tile_ref):
    row = lax.broadcasted_iota(jnp.int32, (BLK, BLK), 0)
    col = lax.broadcasted_iota(jnp.int32, (BLK, BLK), 1)

    def one_group(g, _):
        lags = turned_filt[g]
        before = jnp.zeros((BLK, BLK), F32)
        for k in range(NOFF):
            spread = jnp.broadcast_to(lags[k : k + 1], (BLK, BLK))
            here = pltpu.roll(spread, 1, 1, stride=1, stride_axis=0)
            tile = jnp.where(col > row, before, here)
            tile = jnp.where(k < level[g], tile, 0.0)
            tile_ref[g, k * BLK : (k + 1) * BLK, :] = tile.astype(BF16)
            before = here
        return 0

    lax.fori_loop(0, turned_filt.shape[0], one_group, 0)


def main_kernel(
    level, core, tile_ref, dy_own, x_own, pair, later_same, later_other, dx_ref, send_ref, dy_t, x_t, dh_ref
):
    groups = tile_ref.shape[0]
    per_core = dy_own.shape[0] // BLK
    blocks = 2 * per_core
    h = core[0]

    def turn(src, first, lane, i):
        block = src[aligned((first + i) * BLK, BLK), lane]
        return block.T.reshape(groups, CPG, BLK)

    def put_dy(src, base, lane=slice(None)):
        for i in range(per_core):
            turned = turn(src, 0, lane, i)
            at = (base + i) * CPG
            dy_t[:, aligned(at + CPG, CPG), :BLK] = turned
            dy_t[:, aligned(at, CPG), BLK:] = turned

    def put_x(src, first, base, lane=slice(None)):
        for i in range(per_core):
            x_t[:, aligned((base + i) * CPG, CPG), :] = turn(src, first, lane, i)

    mine = aligned(h * LANES, LANES)
    put_dy(dy_own, h * per_core, mine)
    put_dy(pair, (1 - h) * per_core)
    put_dy(later_same, blocks + h * per_core)
    put_dy(later_other, blocks + (1 - h) * per_core)
    put_x(x_own, 0, h * per_core, mine)
    put_x(pair, per_core, (1 - h) * per_core)

    row = lax.broadcasted_iota(jnp.int32, (BLK, BLK), 0)
    col = lax.broadcasted_iota(jnp.int32, (BLK, BLK), 1)
    within = row + col >= BLK - 1
    flip = jnp.where(row + col == BLK - 1, 1.0, 0.0).astype(BF16)

    def one_group(g, _):
        count = level[g]
        x_flip = lax.dot_general(
            flip, x_t[g], (((1,), (1,)), ((), ())), preferred_element_type=F32
        ).astype(BF16)
        acc = jnp.zeros((blocks * CPG, BLK), F32)
        held = []

        def diagonals(k):
            now = jnp.where(k < count, held[k], 0.0)
            after = jnp.where(k + 1 < count, held[k + 1], 0.0) if k + 1 < NOFF else 0.0
            skew = pltpu.roll(jnp.where(within, now, after), 1, 1, stride=1, stride_axis=0)
            dh_ref[g, k] = jnp.sum(skew.reshape(BLK // 8, 8, BLK), axis=0)

        for two in range(0, NOFF, 2):
            window = dy_t[g, CPG + two * CPG : CPG + (two + blocks) * CPG, :]
            tile = tile_ref[g, two * BLK : (two + 2) * BLK, :]
            acc = acc + jnp.dot(window, tile, preferred_element_type=F32)
            product = jnp.dot(x_flip, window, preferred_element_type=F32)
            held += [product[:, :BLK], product[:, BLK:]]
            if two:
                diagonals(two - 1)
            diagonals(two)
        diagonals(NOFF - 1)
        dx_ref[:, aligned(g * CPG, CPG), :] = acc.reshape(blocks, CPG, BLK).astype(BF16)
        return 0

    lax.fori_loop(0, groups, one_group, 0)

    sums = jnp.sum(dh_ref[...], axis=2)
    lane = lax.broadcasted_iota(jnp.int32, (NOFF, LANES), 1) // QUART
    for q in range(4):
        for p in range(groups // 4):
            packed = jnp.zeros((NOFF, LANES), F32)
            for m in range(4):
                moved = pltpu.roll(sums[4 * p + m], (m - q) % 4 * QUART, 1)
                packed = jnp.where(lane == m, moved, packed)
            send_ref[:, q * (groups // 4) + p, :] = packed


def filter_kernel(scale, got, out):
    total = jnp.sum(got[...], axis=0) * scale
    for i in range(4):
        for m in range(4):
            out[4 * i + m : 4 * i + m + 1, :] = total[i : i + 1, m * QUART : (m + 1) * QUART]


def widen_kernel(got, out):
    cores = 2
    grps = got.shape[0] // cores
    for h in range(cores):
        for r in range(grps):
            at = (r * cores + h) * LANES
            out[:, at : at + LANES] = got[h * grps + r].T


def call(kernel, name, outs, in_specs, scratch=()):
    return pl.pallas_call(
        kernel,
        out_shape=outs,
        in_specs=in_specs,
        out_specs=jax.tree.map(lambda _: VMEM, outs),
        scratch_shapes=scratch,
        compiler_params=PARAMS,
        name=name,
    )


def per_device(inputs, out_grad, filt, band):
    rows, channels = inputs.shape
    groups = channels // CPG // 2
    blocks = 2 * rows // BLK
    chips = lax.axis_size("chip")
    h = lax.axis_index("core")
    seq = ("chip", "core")

    def lanes(whole, which):
        return lax.dynamic_slice_in_dim(whole, which * LANES, LANES, 1)

    def earlier_chip(block, swap):
        pairs = [(2 * c + o, 2 * (c - 1) + (o ^ swap)) for c in range(1, chips) for o in range(2)]
        return lax.ppermute(block, seq, pairs)

    def other_core(block):
        return lax.ppermute(block, "core", [(0, 1), (1, 0)])

    give = lanes(out_grad, 1 - h)
    later_same = earlier_chip(lanes(out_grad, h), 0)
    later_other = earlier_chip(give, 1)
    pair = other_core(jnp.concatenate([give, lanes(inputs, 1 - h)], axis=0))

    level = lax.dynamic_slice_in_dim(jnp.sum(band, axis=1), h * groups, groups, 0)
    my_filt = lax.dynamic_slice_in_dim(filt, h * groups, groups, 0)
    turned = my_filt.reshape(groups, NOFF, BLK)[:, :, ::-1].astype(F32)
    tile = call(
        tiles_kernel,
        "tiles",
        jax.ShapeDtypeStruct((groups, NOFF * BLK, BLK), BF16),
        [SMEM, VMEM],
    )(level, turned)
    dx, send = call(
        main_kernel,
        "main",
        (
            jax.ShapeDtypeStruct((blocks, LANES, BLK), BF16),
            jax.ShapeDtypeStruct((NOFF, groups, LANES), F32),
        ),
        [SMEM, SMEM] + [VMEM] * 6,
        [
            pltpu.VMEM((groups, (2 * blocks + 1) * CPG, 2 * BLK), BF16),
            pltpu.VMEM((groups, blocks * CPG, BLK), BF16),
            pltpu.VMEM((groups, NOFF, 8, BLK), F32),
        ],
    )(level, h[None], tile, out_grad, inputs, pair, later_same, later_other)

    got = lax.all_to_all(send.reshape(2 * chips, groups // 4, LANES), seq, 0, 0, tiled=True)
    wide = lax.all_to_all(dx, ("core", "grp"), 0, 0, tiled=True)
    scale = 1.0 / math.sqrt(rows * 2 * chips * CPG)
    filter_grad = call(
        functools.partial(filter_kernel, scale),
        "filter",
        jax.ShapeDtypeStruct((2 * groups, QUART), F32),
        [VMEM],
    )(got.reshape(chips, groups // 2, LANES))
    input_grad = call(
        widen_kernel, "widen", jax.ShapeDtypeStruct((BLK, blocks * LANES), BF16), [VMEM]
    )(wide)
    return input_grad, filter_grad


def solution(mesh):
    seq, grp = mesh.shape["seq"], mesh.shape["grp"]
    split = Mesh(mesh.devices.reshape(seq // 2, 2, grp), ("chip", "core", "grp"))
    return jax.shard_map(
        per_device,
        mesh=split,
        in_specs=(
            P(("chip", "core"), "grp"),
            P(("chip", "core"), "grp"),
            P("grp", None),
            P("grp", None),
        ),
        out_specs=(P(("chip", "core", "grp"), None), P("grp", ("chip", "core"))),
        check_vma=False,
    )
```

```python
import functools
import math

import jax
import jax.numpy as jnp
from jax import lax
from jax.experimental import pallas as pl
from jax.experimental.pallas import tpu as pltpu
from jax.sharding import Mesh
from jax.sharding import PartitionSpec as P

CPG = 16
BLK = 128
NOFF = 16
LANES = 128
QUART = 32
BF16 = jnp.bfloat16
F32 = jnp.float32
VMEM = pl.BlockSpec(memory_space=pltpu.VMEM)
SMEM = pl.BlockSpec(memory_space=pltpu.SMEM)
PARAMS = pltpu.CompilerParams(vmem_limit_bytes=24 << 20)


def aligned(start, size):
    return pl.ds(pl.multiple_of(start, size), size)


def tiles_kernel(level, turned_filt, tile_ref):
    row = lax.broadcasted_iota(jnp.int32, (BLK, BLK), 0)
    col = lax.broadcasted_iota(jnp.int32, (BLK, BLK), 1)

    def one_group(g, _):
        lags = turned_filt[g]
        before = jnp.zeros((BLK, BLK), F32)
        for k in range(NOFF):
            spread = jnp.broadcast_to(lags[k : k + 1], (BLK, BLK))
            here = pltpu.roll(spread, 1, 1, stride=1, stride_axis=0)
            tile = jnp.where(col > row, before, here)
            tile = jnp.where(k < level[g], tile, 0.0)
            tile_ref[g, k * BLK : (k + 1) * BLK, :] = tile.astype(BF16)
            before = here
        return 0

    lax.fori_loop(0, turned_filt.shape[0], one_group, 0)


def transposed(block):
    return block.T.reshape(-1, CPG, BLK)


def cut_kernel(core, dy, x, keep, give, pair):
    h = core[0]
    rows = dy.shape[0]
    keep[...] = dy[:, aligned(h * LANES, LANES)]
    theirs = aligned((1 - h) * LANES, LANES)
    give[...] = dy[:, theirs]
    pair[:rows] = dy[:, theirs]
    pair[rows:] = x[:, theirs]


def own_kernel(core, dy_own, x_own, pair, dy_out, x_out):
    per_core = dy_own.shape[0] // BLK
    h = core[0]
    mine = aligned(h * LANES, LANES)
    row = lax.broadcasted_iota(jnp.int32, (BLK, BLK), 0)
    col = lax.broadcasted_iota(jnp.int32, (BLK, BLK), 1)
    flip = jnp.where(row + col == BLK - 1, 1.0, 0.0).astype(BF16)

    def run(x_t):
        for i in range(per_core):
            here = pl.ds(i * BLK, BLK)
            first = aligned((h * per_core + i) * CPG, CPG)
            second = aligned(((1 - h) * per_core + i) * CPG, CPG)
            dy_out[:, first, :] = transposed(dy_own[here, mine])
            dy_out[:, second, :] = transposed(pair[here, :])
            x_t[:, first, :] = transposed(x_own[here, mine])
            x_t[:, second, :] = transposed(pair[pl.ds((per_core + i) * BLK, BLK), :])
        for g in range(x_t.shape[0]):
            x_out[g] = lax.dot_general(
                flip, x_t[g], (((1,), (1,)), ((), ())), preferred_element_type=F32
            ).astype(BF16)

    pl.run_scoped(run, pltpu.VMEM(dy_out.shape, BF16))


def window(own, later, g, k):
    if k == 0:
        return own[g]
    return jnp.concatenate([own[g, k * CPG :, :], later[g, : k * CPG, :]], axis=0)


def two_windows(own, later, g, k):
    return jnp.concatenate([window(own, later, g, k), window(own, later, g, k + 1)], axis=1)


def filt_grad_kernel(level, core, x_flip, own, later_same, later_other, send_ref, later, dh_ref):
    groups = own.shape[0]
    per_core = later_same.shape[0] // BLK
    h = core[0]
    for i in range(per_core):
        here = pl.ds(i * BLK, BLK)
        later[:, aligned((h * per_core + i) * CPG, CPG), :] = transposed(later_same[here, :])
        later[:, aligned(((1 - h) * per_core + i) * CPG, CPG), :] = transposed(later_other[here, :])
    row = lax.broadcasted_iota(jnp.int32, (BLK, BLK), 0)
    col = lax.broadcasted_iota(jnp.int32, (BLK, BLK), 1)
    within = row + col >= BLK - 1

    def one_group(g, _):
        count = level[g]
        x_here = x_flip[g]
        held = []

        def diagonals(k):
            now = jnp.where(k < count, held[k], 0.0)
            after = jnp.where(k + 1 < count, held[k + 1], 0.0) if k + 1 < NOFF else 0.0
            skew = pltpu.roll(jnp.where(within, now, after), 1, 1, stride=1, stride_axis=0)
            dh_ref[g, k] = jnp.sum(skew.reshape(BLK // 8, 8, BLK), axis=0)

        for two in range(0, NOFF, 2):
            product = jnp.dot(
                x_here, two_windows(own, later, g, two), preferred_element_type=F32
            )
            held += [product[:, :BLK], product[:, BLK:]]
            if two:
                diagonals(two - 1)
            diagonals(two)
        diagonals(NOFF - 1)
        return 0

    lax.fori_loop(0, groups, one_group, 0)

    for g in range(groups):
        send_ref[:, g, :] = jnp.sum(dh_ref[g], axis=1)


def in_grad_kernel(tile_ref, own, later, dx_ref):
    groups = own.shape[0]

    def one_group(g, _):
        acc = None
        for two in range(0, NOFF, 2):
            part = jnp.dot(
                two_windows(own, later, g, two),
                tile_ref[g, two * BLK : (two + 2) * BLK, :],
                preferred_element_type=F32,
            )
            acc = part if acc is None else acc + part
        dx_ref[:, aligned(g * CPG, CPG), :] = acc.reshape(-1, CPG, BLK).astype(BF16)
        return 0

    lax.fori_loop(0, groups, one_group, 0)


def join_kernel(scale, place, mine, theirs, out):
    core, shift = place[0], place[1]
    groups = mine.shape[0]
    for at, part in ((core, mine), (1 - core, theirs)):
        out[aligned(at * groups, groups), :] = pltpu.roll(part[...], shift, 1)[:, :QUART] * scale


def widen_kernel(got, out):
    cores = 2
    grps = got.shape[0] // cores
    for h in range(cores):
        for r in range(grps):
            at = (r * cores + h) * LANES
            out[:, at : at + LANES] = got[h * grps + r].T


def call(kernel, name, outs, in_specs, scratch=()):
    return pl.pallas_call(
        kernel,
        out_shape=outs,
        in_specs=in_specs,
        out_specs=jax.tree.map(lambda _: VMEM, outs),
        scratch_shapes=scratch,
        compiler_params=PARAMS,
        name=name,
    )


def per_device(inputs, out_grad, filt, band):
    rows, channels = inputs.shape
    groups = channels // CPG // 2
    blocks = 2 * rows // BLK
    chips = 2 * lax.axis_size("z")
    h = lax.axis_index("core")
    seq = ("z", "xh", "core")

    def earlier_chip(block, swap):
        pairs = [(2 * c + o, 2 * (c - 1) + (o ^ swap)) for c in range(1, chips) for o in range(2)]
        return lax.ppermute(block, seq, pairs)

    half = jax.ShapeDtypeStruct((rows, LANES), BF16)
    keep, give, pair = call(
        cut_kernel,
        "cut",
        (half, half, jax.ShapeDtypeStruct((2 * rows, LANES), BF16)),
        [SMEM, VMEM, VMEM],
    )(h[None], out_grad, inputs)
    later_same = earlier_chip(keep, 0)
    later_other = earlier_chip(give, 1)
    pair = lax.ppermute(pair, "core", [(0, 1), (1, 0)])

    level = lax.dynamic_slice_in_dim(jnp.sum(band, axis=1), h * groups, groups, 0)
    my_filt = lax.dynamic_slice_in_dim(filt, h * groups, groups, 0)
    turned = my_filt.reshape(groups, NOFF, BLK)[:, :, ::-1].astype(F32)
    tile = call(
        tiles_kernel,
        "tiles",
        jax.ShapeDtypeStruct((groups, NOFF * BLK, BLK), BF16),
        [SMEM, VMEM],
    )(level, turned)
    turned_shape = jax.ShapeDtypeStruct((groups, blocks * CPG, BLK), BF16)
    own, x_flip = call(
        own_kernel,
        "own",
        (turned_shape, jax.ShapeDtypeStruct((groups, BLK, blocks * CPG), BF16)),
        [SMEM] + [VMEM] * 3,
    )(h[None], out_grad, inputs, pair)
    send, later = call(
        filt_grad_kernel,
        "filt_grad",
        (jax.ShapeDtypeStruct((NOFF, groups, LANES), F32), turned_shape),
        [SMEM, SMEM] + [VMEM] * 4,
        [pltpu.VMEM((groups, NOFF, 8, BLK), F32)],
    )(level, h[None], x_flip, own, later_same, later_other)
    dx = call(
        in_grad_kernel,
        "in_grad",
        jax.ShapeDtypeStruct((blocks, LANES, BLK), BF16),
        [VMEM] * 3,
    )(tile, own, later)

    got = lax.all_to_all(send, "z", 0, 0, tiled=True)
    wide = lax.all_to_all(dx, ("core", "grp"), 0, 0, tiled=True)
    swap = [(0, 1), (1, 0)]
    total = jnp.sum(got, axis=0)
    total = total + lax.ppermute(total, "xh", swap)
    theirs = lax.ppermute(total, "core", swap)
    shift = (LANES - (2 * lax.axis_index("xh") + h) * QUART) % LANES
    scale = 1.0 / math.sqrt(rows * 2 * chips * CPG)
    filter_grad = call(
        functools.partial(join_kernel, scale),
        "join",
        jax.ShapeDtypeStruct((2 * groups, QUART), F32),
        [SMEM, VMEM, VMEM],
    )(jnp.stack([h, shift]), total, theirs)
    input_grad = call(
        widen_kernel, "widen", jax.ShapeDtypeStruct((BLK, blocks * LANES), BF16), [VMEM]
    )(wide)
    return input_grad, filter_grad


def solution(mesh):
    seq, grp = mesh.shape["seq"], mesh.shape["grp"]
    split = Mesh(mesh.devices.reshape(seq // 4, 2, 2, grp), ("z", "xh", "core", "grp"))
    tokens = ("z", "xh", "core")
    return jax.shard_map(
        per_device,
        mesh=split,
        in_specs=(P(tokens, "grp"), P(tokens, "grp"), P("grp", None), P("grp", None)),
        out_specs=(P(tokens + ("grp",), None), P("grp", tokens)),
        check_vma=False,
    )
```

```python
import functools
import math

import jax
import jax.numpy as jnp
from jax import lax
from jax.experimental import pallas as pl
from jax.experimental.pallas import tpu as pltpu
from jax.sharding import Mesh
from jax.sharding import PartitionSpec as P

CPG = 16
BLK = 128
NOFF = 16
LANES = 128
QUART = 32
BF16 = jnp.bfloat16
F32 = jnp.float32
VMEM = pl.BlockSpec(memory_space=pltpu.VMEM)
HBM = pl.BlockSpec(memory_space=pltpu.HBM)
SMEM = pl.BlockSpec(memory_space=pltpu.SMEM)
PARAMS = pltpu.CompilerParams(vmem_limit_bytes=24 << 20)


def aligned(start, size):
    return pl.ds(pl.multiple_of(start, size), size)


def transposed(block):
    return block.T.reshape(-1, CPG, BLK)


def run_copies(sems, *pairs):
    copies = [pltpu.make_async_copy(src, dst, sems.at[i]) for i, (src, dst) in enumerate(pairs)]
    for copy in copies:
        copy.start()
    for copy in copies:
        copy.wait()


def cut_kernel(core, dy, mine, theirs, sems):
    h = core[0]
    run_copies(
        sems,
        (dy.at[:, aligned(h * LANES, LANES)], mine),
        (dy.at[:, aligned((1 - h) * LANES, LANES)], theirs),
    )


def pack_kernel(core, x, dy_theirs, mine, pair, sems):
    h = core[0]
    rows = x.shape[0]
    run_copies(
        sems,
        (x.at[:, aligned(h * LANES, LANES)], mine),
        (dy_theirs, pair.at[:rows]),
        (x.at[:, aligned((1 - h) * LANES, LANES)], pair.at[rows:]),
    )


def own_kernel(core, dy_own, x_own, pair, dy_out, x_out):
    per_core = dy_own.shape[0] // BLK
    h = core[0]
    row = lax.broadcasted_iota(jnp.int32, (BLK, BLK), 0)
    col = lax.broadcasted_iota(jnp.int32, (BLK, BLK), 1)
    flip = jnp.where(row + col == BLK - 1, 1.0, 0.0).astype(BF16)

    def run(x_t):
        for i in range(per_core):
            here = pl.ds(i * BLK, BLK)
            first = aligned((h * per_core + i) * CPG, CPG)
            second = aligned(((1 - h) * per_core + i) * CPG, CPG)
            dy_out[:, first, :] = transposed(dy_own[here, :])
            dy_out[:, second, :] = transposed(pair[here, :])
            x_t[:, first, :] = transposed(x_own[here, :])
            x_t[:, second, :] = transposed(pair[pl.ds((per_core + i) * BLK, BLK), :])
        for g in range(x_t.shape[0]):
            x_out[g] = lax.dot_general(
                flip, x_t[g], (((1,), (1,)), ((), ())), preferred_element_type=F32
            ).astype(BF16)

    pl.run_scoped(run, pltpu.VMEM(dy_out.shape, BF16))


def window(own, later, g, k):
    if k == 0:
        return own[g]
    return jnp.concatenate([own[g, k * CPG :, :], later[g, : k * CPG, :]], axis=0)


def two_windows(own, later, g, k):
    return jnp.concatenate([window(own, later, g, k), window(own, later, g, k + 1)], axis=1)


def filt_grad_kernel(level, core, x_flip, own, later_same, later_other, send_ref, later, dh_ref):
    groups = own.shape[0]
    per_core = later_same.shape[0] // BLK
    h = core[0]
    for i in range(per_core):
        here = pl.ds(i * BLK, BLK)
        later[:, aligned((h * per_core + i) * CPG, CPG), :] = transposed(later_same[here, :])
        later[:, aligned(((1 - h) * per_core + i) * CPG, CPG), :] = transposed(later_other[here, :])
    row = lax.broadcasted_iota(jnp.int32, (BLK, BLK), 0)
    col = lax.broadcasted_iota(jnp.int32, (BLK, BLK), 1)
    within = row + col >= BLK - 1

    for g in range(groups):
        count = level[g]

        def diagonals(k, now, after):
            after = 0.0 if after is None else jnp.where(k + 1 < count, after, 0.0)
            skew = pltpu.roll(jnp.where(within, now, after), 1, 1, stride=1, stride_axis=0)
            eight = jnp.sum(skew.reshape(BLK // 8, 8, BLK), axis=0)
            dh_ref[k, g] = jnp.where(k < count, eight, 0.0)

        last = None
        for two in range(0, NOFF, 2):
            product = jnp.dot(
                x_flip[g], two_windows(own, later, g, two), preferred_element_type=F32
            )
            now, after = product[:, :BLK], product[:, BLK:]
            if two:
                diagonals(two - 1, last, now)
            diagonals(two, now, after)
            last = after
        diagonals(NOFF - 1, last, None)

    sub = lax.broadcasted_iota(jnp.int32, (8, BLK), 0)
    for k in range(NOFF):
        send_ref[k] = column_sums([dh_ref[k, g] for g in range(groups)], sub)


def column_sums(parts, sub):
    for step in (4, 2, 1):
        low = sub % (2 * step) < step
        half = len(parts) // 2
        parts = [
            jnp.where(low, a, b) + pltpu.roll(jnp.where(low, b, a), step, 0)
            if step == 4
            else jnp.where(low, a + pltpu.roll(a, 8 - step, 0), b + pltpu.roll(b, step, 0))
            for a, b in zip(parts[:half], parts[half:])
        ]
    return parts[0]


def in_grad_kernel(level, turned_filt, own, later, dx_ref):
    row = lax.broadcasted_iota(jnp.int32, (BLK, BLK), 0)
    col = lax.broadcasted_iota(jnp.int32, (BLK, BLK), 1)

    def one_group(g, _):
        lags = turned_filt[g]
        before = jnp.zeros((BLK, BLK), F32)
        tiles = []
        for k in range(NOFF):
            spread = jnp.broadcast_to(lags[k : k + 1], (BLK, BLK))
            here = pltpu.roll(spread, 1, 1, stride=1, stride_axis=0)
            tile = jnp.where(col > row, before, here)
            tiles.append(jnp.where(k < level[g], tile, 0.0).astype(BF16))
            before = here
        wide = jnp.concatenate([window(own, later, g, k) for k in range(NOFF)], axis=1)
        grad = jnp.dot(wide, jnp.concatenate(tiles, axis=0), preferred_element_type=F32)
        dx_ref[:, aligned(g * CPG, CPG), :] = grad.reshape(-1, CPG, BLK).astype(BF16)
        return 0

    lax.fori_loop(0, own.shape[0], one_group, 0, unroll=8)


def last_kernel(scale, place, got, mine, theirs, wide, narrow):
    cores = 2
    grps = got.shape[0] // cores
    for h in range(cores):
        for r in range(grps):
            at = (r * cores + h) * LANES
            wide[:, at : at + LANES] = got[h * grps + r].T
    core, shift = place[0], place[1]
    groups = mine.shape[0]
    for at, part in ((core, mine), (1 - core, theirs)):
        narrow[aligned(at * groups, groups), :] = pltpu.roll(part[...], shift, 1)[:, :QUART] * scale


def call(kernel, name, outs, in_specs, scratch=()):
    return pl.pallas_call(
        kernel,
        out_shape=outs,
        in_specs=in_specs,
        out_specs=jax.tree.map(lambda _: VMEM, outs),
        scratch_shapes=scratch,
        compiler_params=PARAMS,
        name=name,
    )


def per_device(inputs, out_grad, filt, band):
    rows, channels = inputs.shape
    groups = channels // CPG // 2
    blocks = 2 * rows // BLK
    chips = 2 * lax.axis_size("z")
    h = lax.axis_index("core")
    seq = ("z", "xh", "core")

    def earlier_chip(block, swap):
        pairs = [(2 * c + o, 2 * (c - 1) + (o ^ swap)) for c in range(1, chips) for o in range(2)]
        return lax.ppermute(block, seq, pairs)

    half = jax.ShapeDtypeStruct((rows, LANES), BF16)

    dy_mine, dy_theirs = call(
        cut_kernel, "cut", (half, half), [SMEM, HBM], [pltpu.SemaphoreType.DMA((2,))]
    )(h[None], out_grad)
    later_same = earlier_chip(dy_mine, 0)
    later_other = earlier_chip(dy_theirs, 1)
    x_mine, pair = call(
        pack_kernel,
        "pack",
        (half, jax.ShapeDtypeStruct((2 * rows, LANES), BF16)),
        [SMEM, HBM, VMEM],
        [pltpu.SemaphoreType.DMA((3,))],
    )(h[None], inputs, dy_theirs)
    swap = [(0, 1), (1, 0)]
    pair = lax.ppermute(pair, "core", swap)
    level = lax.dynamic_slice_in_dim(jnp.sum(band, axis=1), h * groups, groups, 0)
    my_filt = lax.dynamic_slice_in_dim(filt, h * groups, groups, 0)
    turned = my_filt.reshape(groups, NOFF, BLK)[:, :, ::-1].astype(F32)
    turned_shape = jax.ShapeDtypeStruct((groups, blocks * CPG, BLK), BF16)
    own, x_flip = call(
        own_kernel,
        "own",
        (turned_shape, jax.ShapeDtypeStruct((groups, BLK, blocks * CPG), BF16)),
        [SMEM] + [VMEM] * 3,
    )(h[None], dy_mine, x_mine, pair)
    send, later = call(
        filt_grad_kernel,
        "filt_grad",
        (jax.ShapeDtypeStruct((NOFF, groups, LANES), F32), turned_shape),
        [SMEM, SMEM] + [VMEM] * 4,
        [pltpu.VMEM((NOFF, groups, 8, BLK), F32)],
    )(level, h[None], x_flip, own, later_same, later_other)
    dx = call(
        in_grad_kernel,
        "in_grad",
        jax.ShapeDtypeStruct((blocks, LANES, BLK), BF16),
        [SMEM] + [VMEM] * 3,
    )(level, turned, own, later)

    got = lax.all_to_all(send, "z", 0, 0, tiled=True)
    wide = lax.all_to_all(dx, ("core", "grp"), 0, 0, tiled=True)
    total = jnp.sum(got, axis=0)
    total = total + lax.ppermute(total, "xh", swap)
    theirs = lax.ppermute(total, "core", swap)
    shift = (LANES - (2 * lax.axis_index("xh") + h) * QUART) % LANES
    scale = 1.0 / math.sqrt(rows * 2 * chips * CPG)
    return call(
        functools.partial(last_kernel, scale),
        "last",
        (
            jax.ShapeDtypeStruct((BLK, blocks * LANES), BF16),
            jax.ShapeDtypeStruct((2 * groups, QUART), F32),
        ),
        [SMEM] + [VMEM] * 3,
    )(jnp.stack([h, shift]), wide, total, theirs)


def solution(mesh):
    seq, grp = mesh.shape["seq"], mesh.shape["grp"]
    split = Mesh(mesh.devices.reshape(seq // 4, 2, 2, grp), ("z", "xh", "core", "grp"))
    tokens = ("z", "xh", "core")
    return jax.shard_map(
        per_device,
        mesh=split,
        in_specs=(P(tokens, "grp"), P(tokens, "grp"), P("grp", None), P("grp", None)),
        out_specs=(P(tokens + ("grp",), None), P("grp", tokens)),
        check_vma=False,
    )
```

```python
import functools
import math

import jax
import jax.numpy as jnp
from jax import lax
from jax.experimental import pallas as pl
from jax.experimental.pallas import tpu as pltpu
from jax.sharding import Mesh
from jax.sharding import PartitionSpec as P

CPG = 16
BLK = 128
NOFF = 16
LANES = 128
QUART = 32
BF16 = jnp.bfloat16
F32 = jnp.float32
VMEM = pl.BlockSpec(memory_space=pltpu.VMEM)
SMEM = pl.BlockSpec(memory_space=pltpu.SMEM)
PARAMS = pltpu.CompilerParams(vmem_limit_bytes=24 << 20)


def aligned(start, size):
    return pl.ds(pl.multiple_of(start, size), size)


def transposed(block):
    return block.T.reshape(-1, CPG, BLK)


def turn(core, whole, gathered, out):
    per_core = whole.shape[0] // BLK
    mine = aligned(core * LANES, LANES)
    for i in range(per_core):
        here = pl.ds(i * BLK, BLK)
        out[:, aligned((core * per_core + i) * CPG, CPG), :] = transposed(whole[here, mine])
        other = transposed(gathered[1 - core, here, :])
        out[:, aligned(((1 - core) * per_core + i) * CPG, CPG), :] = other


def own_kernel(core, dy, dy_gathered, x, x_gathered, dy_out, x_out, x_t):
    row = lax.broadcasted_iota(jnp.int32, (BLK, BLK), 0)
    col = lax.broadcasted_iota(jnp.int32, (BLK, BLK), 1)
    flip = jnp.where(row + col == BLK - 1, 1.0, 0.0).astype(BF16)
    turn(core[0], dy, dy_gathered, dy_out)
    turn(core[0], x, x_gathered, x_t)
    for g in range(x_t.shape[0]):
        x_out[g] = lax.dot_general(
            flip, x_t[g], (((1,), (1,)), ((), ())), preferred_element_type=F32
        ).astype(BF16)


def window(own, later, g, k):
    if k == 0:
        return own[g]
    return jnp.concatenate([own[g, k * CPG :, :], later[g, : k * CPG, :]], axis=0)


def two_windows(own, later, g, k):
    return jnp.concatenate([window(own, later, g, k), window(own, later, g, k + 1)], axis=1)


def filt_grad_kernel(level, core, x_flip, own, dy, dy_gathered, send_ref, later, dh_ref):
    groups = own.shape[0]
    turn(core[0], dy, dy_gathered, later)
    row = lax.broadcasted_iota(jnp.int32, (BLK, BLK), 0)
    col = lax.broadcasted_iota(jnp.int32, (BLK, BLK), 1)
    within = row + col >= BLK - 1

    for g in range(groups):
        count = level[g]

        def diagonals(k, now, after):
            after = 0.0 if after is None else jnp.where(k + 1 < count, after, 0.0)
            skew = pltpu.roll(jnp.where(within, now, after), 1, 1, stride=1, stride_axis=0)
            eight = jnp.sum(skew.reshape(BLK // 8, 8, BLK), axis=0)
            dh_ref[k, g] = jnp.where(k < count, eight, 0.0)

        last = None
        for two in range(0, NOFF, 2):
            product = jnp.dot(
                x_flip[g], two_windows(own, later, g, two), preferred_element_type=F32
            )
            now, after = product[:, :BLK], product[:, BLK:]
            if two:
                diagonals(two - 1, last, now)
            diagonals(two, now, after)
            last = after
        diagonals(NOFF - 1, last, None)

    sub = lax.broadcasted_iota(jnp.int32, (8, BLK), 0)
    for k in range(NOFF):
        send_ref[k] = column_sums([dh_ref[k, g] for g in range(groups)], sub)


def column_sums(parts, sub):
    for step in (4, 2, 1):
        low = sub % (2 * step) < step
        half = len(parts) // 2
        parts = [
            jnp.where(low, a, b) + pltpu.roll(jnp.where(low, b, a), step, 0)
            if step == 4
            else jnp.where(low, a + pltpu.roll(a, 8 - step, 0), b + pltpu.roll(b, step, 0))
            for a, b in zip(parts[:half], parts[half:])
        ]
    return parts[0]


def in_grad_kernel(level, turned_filt, own, later, dx_ref):
    row = lax.broadcasted_iota(jnp.int32, (BLK, BLK), 0)
    col = lax.broadcasted_iota(jnp.int32, (BLK, BLK), 1)

    def one_group(g, _):
        lags = turned_filt[g]
        before = jnp.zeros((BLK, BLK), F32)
        tiles = []
        for k in range(NOFF):
            spread = jnp.broadcast_to(lags[k : k + 1], (BLK, BLK))
            here = pltpu.roll(spread, 1, 1, stride=1, stride_axis=0)
            tile = jnp.where(col > row, before, here)
            tiles.append(jnp.where(k < level[g], tile, 0.0).astype(BF16))
            before = here
        wide = jnp.concatenate([window(own, later, g, k) for k in range(NOFF)], axis=1)
        grad = jnp.dot(wide, jnp.concatenate(tiles, axis=0), preferred_element_type=F32)
        dx_ref[:, aligned(g * CPG, CPG), :] = grad.reshape(-1, CPG, BLK).astype(BF16)
        return 0

    lax.fori_loop(0, own.shape[0], one_group, 0, unroll=8)


def last_kernel(scale, shift, got, parts, wide, narrow):
    cores = 2
    grps = got.shape[0] // cores
    groups = parts.shape[1]
    for h in range(cores):
        for r in range(grps):
            at = (r * cores + h) * LANES
            wide[:, at : at + LANES] = got[h * grps + r].T
        total = parts[h] + parts[cores + h]
        lags = pltpu.roll(total, shift[0], 1)[:, :QUART]
        narrow[h * groups : (h + 1) * groups, :] = lags * scale


def call(kernel, name, outs, in_specs, scratch=()):
    return pl.pallas_call(
        kernel,
        out_shape=outs,
        in_specs=in_specs,
        out_specs=jax.tree.map(lambda _: VMEM, outs),
        scratch_shapes=scratch,
        compiler_params=PARAMS,
        name=name,
    )


def per_device(inputs, out_grad, filt, band):
    rows, channels = inputs.shape
    groups = channels // CPG // 2
    blocks = 2 * rows // BLK
    chips = 2 * lax.axis_size("z")
    h = lax.axis_index("core")
    seq = ("z", "xh", "core")

    def swapped(whole):
        theirs = lax.dynamic_slice_in_dim(whole, (1 - h) * LANES, LANES, 1)
        return lax.all_gather(theirs, "core")

    later_dy = lax.ppermute(out_grad, seq, [(i, i - 2) for i in range(2, 2 * chips)])

    level = lax.dynamic_slice_in_dim(jnp.sum(band, axis=1), h * groups, groups, 0)
    my_filt = lax.dynamic_slice_in_dim(filt, h * groups, groups, 0)
    turned = my_filt.reshape(groups, NOFF, BLK)[:, :, ::-1].astype(F32)
    turned_shape = jax.ShapeDtypeStruct((groups, blocks * CPG, BLK), BF16)
    own, x_flip = call(
        own_kernel,
        "own",
        (turned_shape, jax.ShapeDtypeStruct((groups, BLK, blocks * CPG), BF16)),
        [SMEM] + [VMEM] * 4,
        [pltpu.VMEM(turned_shape.shape, BF16)],
    )(h[None], out_grad, swapped(out_grad), inputs, swapped(inputs))
    send, later = call(
        filt_grad_kernel,
        "filt_grad",
        (jax.ShapeDtypeStruct((NOFF, groups, LANES), F32), turned_shape),
        [SMEM, SMEM] + [VMEM] * 4,
        [pltpu.VMEM((NOFF, groups, 8, BLK), F32)],
    )(level, h[None], x_flip, own, later_dy, swapped(later_dy))
    dx = call(
        in_grad_kernel,
        "in_grad",
        jax.ShapeDtypeStruct((blocks, LANES, BLK), BF16),
        [SMEM] + [VMEM] * 3,
    )(level, turned, own, later)

    got = lax.all_to_all(send, "z", 0, 0, tiled=True)
    wide = lax.all_to_all(dx, ("core", "grp"), 0, 0, tiled=True)
    parts = lax.all_gather(jnp.sum(got, axis=0), ("xh", "core"))
    shift = (LANES - (2 * lax.axis_index("xh") + h) * QUART) % LANES
    scale = 1.0 / math.sqrt(rows * 2 * chips * CPG)
    return call(
        functools.partial(last_kernel, scale),
        "last",
        (
            jax.ShapeDtypeStruct((BLK, blocks * LANES), BF16),
            jax.ShapeDtypeStruct((2 * groups, QUART), F32),
        ),
        [SMEM] + [VMEM] * 2,
    )(shift[None], wide, parts)


def solution(mesh):
    seq, grp = mesh.shape["seq"], mesh.shape["grp"]
    split = Mesh(mesh.devices.reshape(seq // 4, 2, 2, grp), ("z", "xh", "core", "grp"))
    tokens = ("z", "xh", "core")
    return jax.shard_map(
        per_device,
        mesh=split,
        in_specs=(P(tokens, "grp"), P(tokens, "grp"), P("grp", None), P("grp", None)),
        out_specs=(P(tokens + ("grp",), None), P("grp", tokens)),
        check_vma=False,
    )
```

```python
import functools
import math

import jax
import jax.numpy as jnp
from jax import lax
from jax.experimental import pallas as pl
from jax.experimental.pallas import tpu as pltpu
from jax.sharding import Mesh
from jax.sharding import PartitionSpec as P

CPG = 16
BLK = 128
NOFF = 16
LANES = 128
QUART = 32
BF16 = jnp.bfloat16
F32 = jnp.float32
VMEM = pl.BlockSpec(memory_space=pltpu.VMEM)
SMEM = pl.BlockSpec(memory_space=pltpu.SMEM)
PARAMS = pltpu.CompilerParams(vmem_limit_bytes=24 << 20)


def aligned(start, size):
    return pl.ds(pl.multiple_of(start, size), size)


def transposed(block):
    return block.T.reshape(-1, CPG, BLK)


def turn(core, whole, gathered, out):
    per_core = whole.shape[0] // BLK
    mine = aligned(core * LANES, LANES)
    for i in range(per_core):
        here = pl.ds(i * BLK, BLK)
        out[:, aligned((core * per_core + i) * CPG, CPG), :] = transposed(whole[here, mine])
        other = transposed(gathered[1 - core, here, :])
        out[:, aligned(((1 - core) * per_core + i) * CPG, CPG), :] = other


def own_kernel(core, dy, dy_gathered, x, x_gathered, dy_out, x_out, x_t):
    row = lax.broadcasted_iota(jnp.int32, (BLK, BLK), 0)
    col = lax.broadcasted_iota(jnp.int32, (BLK, BLK), 1)
    flip = jnp.where(row + col == BLK - 1, 1.0, 0.0).astype(BF16)
    turn(core[0], dy, dy_gathered, dy_out)
    turn(core[0], x, x_gathered, x_t)
    for g in range(x_t.shape[0]):
        x_out[g] = lax.dot_general(
            flip, x_t[g], (((1,), (1,)), ((), ())), preferred_element_type=F32
        ).astype(BF16)


def window(own, later, g, k):
    if k == 0:
        return own[g]
    return jnp.concatenate([own[g, k * CPG :, :], later[g, : k * CPG, :]], axis=0)


def two_windows(own, later, g, k):
    return jnp.concatenate([window(own, later, g, k), window(own, later, g, k + 1)], axis=1)


def filt_grad_kernel(level, core, x_flip, own, dy, dy_gathered, send_ref, later, dh_ref):
    groups = own.shape[0]
    turn(core[0], dy, dy_gathered, later)
    row = lax.broadcasted_iota(jnp.int32, (BLK, BLK), 0)
    col = lax.broadcasted_iota(jnp.int32, (BLK, BLK), 1)
    within = row + col >= BLK - 1

    for g in range(groups):
        count = level[g]

        def diagonals(k, now, after):
            after = 0.0 if after is None else jnp.where(k + 1 < count, after, 0.0)
            skew = pltpu.roll(jnp.where(within, now, after), 1, 1, stride=1, stride_axis=0)
            eight = jnp.sum(skew.reshape(BLK // 8, 8, BLK), axis=0)
            dh_ref[k, g] = jnp.where(k < count, eight, 0.0)

        last = None
        for two in range(0, NOFF, 2):
            product = jnp.dot(
                x_flip[g], two_windows(own, later, g, two), preferred_element_type=F32
            )
            now, after = product[:, :BLK], product[:, BLK:]
            if two:
                diagonals(two - 1, last, now)
            diagonals(two, now, after)
            last = after
        diagonals(NOFF - 1, last, None)

    sub = lax.broadcasted_iota(jnp.int32, (8, BLK), 0)
    for k in range(NOFF):
        send_ref[k] = column_sums([dh_ref[k, g] for g in range(groups)], sub)


def column_sums(parts, sub):
    for step in (4, 2, 1):
        low = sub % (2 * step) < step
        half = len(parts) // 2
        parts = [
            jnp.where(low, a, b) + pltpu.roll(jnp.where(low, b, a), step, 0)
            if step == 4
            else jnp.where(low, a + pltpu.roll(a, 8 - step, 0), b + pltpu.roll(b, step, 0))
            for a, b in zip(parts[:half], parts[half:])
        ]
    return parts[0]


def in_grad_kernel(level, core, turned_filt, own, later, mine, theirs):
    row = lax.broadcasted_iota(jnp.int32, (BLK, BLK), 0)
    col = lax.broadcasted_iota(jnp.int32, (BLK, BLK), 1)
    first = core[0] == 0

    def one_group(g, _):
        lags = turned_filt[g]
        before = jnp.zeros((BLK, BLK), F32)
        tiles = []
        for k in range(NOFF):
            spread = jnp.broadcast_to(lags[k : k + 1], (BLK, BLK))
            here = pltpu.roll(spread, 1, 1, stride=1, stride_axis=0)
            tile = jnp.where(col > row, before, here)
            tiles.append(jnp.where(k < level[g], tile, 0.0).astype(BF16))
            before = here
        wide = jnp.concatenate([window(own, later, g, k) for k in range(NOFF)], axis=1)
        grad = jnp.dot(wide, jnp.concatenate(tiles, axis=0), preferred_element_type=F32)
        blocks = grad.reshape(2, -1, CPG, BLK).astype(BF16)
        mine[:, aligned(g * CPG, CPG), :] = jnp.where(first, blocks[0], blocks[1])
        theirs[:, aligned(g * CPG, CPG), :] = jnp.where(first, blocks[1], blocks[0])
        return 0

    lax.fori_loop(0, own.shape[0], one_group, 0, unroll=8)


def pack_kernel(core, mine, gathered, out):
    out[:, :LANES, :] = mine[...]
    out[:, LANES:, :] = gathered[1 - core[0]]


def last_kernel(scale, place, got, parts, wide, narrow):
    cores = 2
    groups = parts.shape[1]
    for r in range(got.shape[0]):
        for i, h in enumerate((place[0], 1 - place[0])):
            at = aligned((r * cores + h) * LANES, LANES)
            wide[:, at] = got[r, i * LANES : (i + 1) * LANES, :].T
    for h in range(cores):
        total = parts[h] + parts[cores + h]
        lags = pltpu.roll(total, place[1], 1)[:, :QUART]
        narrow[h * groups : (h + 1) * groups, :] = lags * scale


def call(kernel, name, outs, in_specs, scratch=()):
    return pl.pallas_call(
        kernel,
        out_shape=outs,
        in_specs=in_specs,
        out_specs=jax.tree.map(lambda _: VMEM, outs),
        scratch_shapes=scratch,
        compiler_params=PARAMS,
        name=name,
    )


def per_device(inputs, out_grad, filt, band):
    rows, channels = inputs.shape
    groups = channels // CPG // 2
    blocks = 2 * rows // BLK
    chips = 2 * lax.axis_size("z")
    h = lax.axis_index("core")
    seq = ("z", "xh", "core")

    def swapped(whole):
        theirs = lax.dynamic_slice_in_dim(whole, (1 - h) * LANES, LANES, 1)
        return lax.all_gather(theirs, "core")

    later_dy = lax.ppermute(out_grad, seq, [(i, i - 2) for i in range(2, 2 * chips)])

    level = lax.dynamic_slice_in_dim(jnp.sum(band, axis=1), h * groups, groups, 0)
    my_filt = lax.dynamic_slice_in_dim(filt, h * groups, groups, 0)
    turned = my_filt.reshape(groups, NOFF, BLK)[:, :, ::-1].astype(F32)
    turned_shape = jax.ShapeDtypeStruct((groups, blocks * CPG, BLK), BF16)
    own, x_flip = call(
        own_kernel,
        "own",
        (turned_shape, jax.ShapeDtypeStruct((groups, BLK, blocks * CPG), BF16)),
        [SMEM] + [VMEM] * 4,
        [pltpu.VMEM(turned_shape.shape, BF16)],
    )(h[None], out_grad, swapped(out_grad), inputs, swapped(inputs))
    send, later = call(
        filt_grad_kernel,
        "filt_grad",
        (jax.ShapeDtypeStruct((NOFF, groups, LANES), F32), turned_shape),
        [SMEM, SMEM] + [VMEM] * 4,
        [pltpu.VMEM((NOFF, groups, 8, BLK), F32)],
    )(level, h[None], x_flip, own, later_dy, swapped(later_dy))
    half = jax.ShapeDtypeStruct((blocks // 2, LANES, BLK), BF16)
    mine, theirs = call(
        in_grad_kernel,
        "in_grad",
        (half, half),
        [SMEM] * 2 + [VMEM] * 3,
    )(level, h[None], turned, own, later)
    dx = call(
        pack_kernel,
        "pack",
        jax.ShapeDtypeStruct((blocks // 2, 2 * LANES, BLK), BF16),
        [SMEM] + [VMEM] * 2,
    )(h[None], mine, lax.all_gather(theirs, "core"))

    got = lax.all_to_all(send, "z", 0, 0, tiled=True)
    wide = lax.all_to_all(dx, "grp", 0, 0, tiled=True)
    parts = lax.all_gather(jnp.sum(got, axis=0), ("xh", "core"))
    shift = (LANES - (2 * lax.axis_index("xh") + h) * QUART) % LANES
    scale = 1.0 / math.sqrt(rows * 2 * chips * CPG)
    return call(
        functools.partial(last_kernel, scale),
        "last",
        (
            jax.ShapeDtypeStruct((BLK, blocks * LANES), BF16),
            jax.ShapeDtypeStruct((2 * groups, QUART), F32),
        ),
        [SMEM] + [VMEM] * 2,
    )(jnp.stack([h, shift]), wide, parts)


def solution(mesh):
    seq, grp = mesh.shape["seq"], mesh.shape["grp"]
    split = Mesh(mesh.devices.reshape(seq // 4, 2, 2, grp), ("z", "xh", "core", "grp"))
    tokens = ("z", "xh", "core")
    return jax.shard_map(
        per_device,
        mesh=split,
        in_specs=(P(tokens, "grp"), P(tokens, "grp"), P("grp", None), P("grp", None)),
        out_specs=(P(tokens + ("grp",), None), P("grp", tokens)),
        check_vma=False,
    )
```

```python
import functools
import math

import jax
import jax.numpy as jnp
from jax import lax
from jax.experimental import pallas as pl
from jax.experimental.pallas import tpu as pltpu
from jax.sharding import Mesh
from jax.sharding import PartitionSpec as P

CPG = 16
BLK = 128
NOFF = 16
LANES = 128
QUART = 32
BF16 = jnp.bfloat16
F32 = jnp.float32
VMEM = pl.BlockSpec(memory_space=pltpu.VMEM)
SMEM = pl.BlockSpec(memory_space=pltpu.SMEM)
PARAMS = pltpu.CompilerParams(vmem_limit_bytes=24 << 20)


def aligned(start, size):
    return pl.ds(pl.multiple_of(start, size), size)


def transposed(block):
    return block.T.reshape(-1, CPG, BLK)


def turn(core, whole, gathered, out):
    per_core = whole.shape[0] // BLK
    mine = aligned(core * LANES, LANES)
    for i in range(per_core):
        here = pl.ds(i * BLK, BLK)
        out[:, aligned((core * per_core + i) * CPG, CPG), :] = transposed(whole[here, mine])
        other = transposed(gathered[1 - core, here, :])
        out[:, aligned(((1 - core) * per_core + i) * CPG, CPG), :] = other


def own_kernel(core, dy, dy_gathered, x, x_gathered, dy_out, x_out, x_t):
    row = lax.broadcasted_iota(jnp.int32, (BLK, BLK), 0)
    col = lax.broadcasted_iota(jnp.int32, (BLK, BLK), 1)
    flip = jnp.where(row + col == BLK - 1, 1.0, 0.0).astype(BF16)
    turn(core[0], dy, dy_gathered, dy_out)
    turn(core[0], x, x_gathered, x_t)
    for g in range(x_t.shape[0]):
        x_out[g] = lax.dot_general(
            flip, x_t[g], (((1,), (1,)), ((), ())), preferred_element_type=F32
        ).astype(BF16)


def window(own, later, g, k):
    if k == 0:
        return own[g]
    return jnp.concatenate([own[g, k * CPG :, :], later[g, : k * CPG, :]], axis=0)


def two_windows(own, later, g, k):
    return jnp.concatenate([window(own, later, g, k), window(own, later, g, k + 1)], axis=1)


def filt_grad_kernel(core, level, x_flip, own, dy, dy_gathered, send_ref, later, dh_ref):
    groups = own.shape[0]
    turn(core[0], dy, dy_gathered, later)
    row = lax.broadcasted_iota(jnp.int32, (BLK, BLK), 0)
    col = lax.broadcasted_iota(jnp.int32, (BLK, BLK), 1)
    within = row + col >= BLK - 1

    for g in range(groups):
        count = level[g : g + 1, :]

        def diagonals(k, now, after):
            after = 0.0 if after is None else jnp.where(k + 1 < count, after, 0.0)
            skew = pltpu.roll(jnp.where(within, now, after), 1, 1, stride=1, stride_axis=0)
            eight = jnp.sum(skew.reshape(BLK // 8, 8, BLK), axis=0)
            dh_ref[k, g] = jnp.where(k < count, eight, 0.0)

        last = None
        for two in range(0, NOFF, 2):
            product = jnp.dot(
                x_flip[g], two_windows(own, later, g, two), preferred_element_type=F32
            )
            now, after = product[:, :BLK], product[:, BLK:]
            if two:
                diagonals(two - 1, last, now)
            diagonals(two, now, after)
            last = after
        diagonals(NOFF - 1, last, None)

    sub = lax.broadcasted_iota(jnp.int32, (8, BLK), 0)
    for k in range(NOFF):
        send_ref[k] = column_sums([dh_ref[k, g] for g in range(groups)], sub)


def column_sums(parts, sub):
    for step in (4, 2, 1):
        low = sub % (2 * step) < step
        half = len(parts) // 2
        parts = [
            jnp.where(low, a, b) + pltpu.roll(jnp.where(low, b, a), step, 0)
            if step == 4
            else jnp.where(low, a + pltpu.roll(a, 8 - step, 0), b + pltpu.roll(b, step, 0))
            for a, b in zip(parts[:half], parts[half:])
        ]
    return parts[0]


def in_grad_kernel(core, level, turned_filt, own, later, mine, theirs):
    row = lax.broadcasted_iota(jnp.int32, (BLK, BLK), 0)
    col = lax.broadcasted_iota(jnp.int32, (BLK, BLK), 1)
    first = core[0] == 0

    def one_group(g, _):
        lags = turned_filt[g]
        count = level[pl.ds(g, 1), :]
        before = jnp.zeros((BLK, BLK), F32)
        tiles = []
        for k in range(NOFF):
            spread = jnp.broadcast_to(lags[k : k + 1], (BLK, BLK))
            here = pltpu.roll(spread, 1, 1, stride=1, stride_axis=0)
            tile = jnp.where(col > row, before, here)
            tiles.append(jnp.where(k < count, tile, 0.0).astype(BF16))
            before = here
        wide = jnp.concatenate([window(own, later, g, k) for k in range(NOFF)], axis=1)
        grad = jnp.dot(wide, jnp.concatenate(tiles, axis=0), preferred_element_type=F32)
        blocks = grad.reshape(2, -1, CPG, BLK).astype(BF16)
        mine[:, aligned(g * CPG, CPG), :] = jnp.where(first, blocks[0], blocks[1])
        theirs[:, aligned(g * CPG, CPG), :] = jnp.where(first, blocks[1], blocks[0])
        return 0

    lax.fori_loop(0, own.shape[0], one_group, 0, unroll=8)


def pack_kernel(core, mine, gathered, out):
    out[:, :LANES, :] = mine[...]
    out[:, LANES:, :] = gathered[1 - core[0]]


def last_kernel(scale, core, shift, got, parts, wide, narrow):
    cores = 2
    groups = parts.shape[1]
    first = core[0] == 0
    for r in range(got.shape[0]):
        mine = got[r, :LANES, :].T
        other = got[r, LANES:, :].T
        at = r * cores * LANES
        wide[:, at : at + LANES] = jnp.where(first, mine, other)
        wide[:, at + LANES : at + 2 * LANES] = jnp.where(first, other, mine)
    for h in range(cores):
        total = parts[h] + parts[cores + h]
        lags = pltpu.roll(total, shift[0], 1)[:, :QUART]
        narrow[h * groups : (h + 1) * groups, :] = lags * scale


def call(kernel, name, outs, in_specs, scratch=()):
    return pl.pallas_call(
        kernel,
        out_shape=outs,
        in_specs=in_specs,
        out_specs=jax.tree.map(lambda _: VMEM, outs),
        scratch_shapes=scratch,
        compiler_params=PARAMS,
        name=name,
    )


def per_device(inputs, out_grad, filt, band):
    rows, channels = inputs.shape
    groups = channels // CPG // 2
    blocks = 2 * rows // BLK
    chips = 2 * lax.axis_size("z")
    h = lax.axis_index("core")
    seq = ("z", "xh", "core")

    def swapped(whole):
        theirs = lax.dynamic_slice_in_dim(whole, (1 - h) * LANES, LANES, 1)
        return lax.all_gather(theirs, "core")

    later_dy = lax.ppermute(out_grad, seq, [(i, i - 2) for i in range(2, 2 * chips)])

    level = lax.dynamic_slice_in_dim(jnp.sum(band, axis=1, keepdims=True), h * groups, groups, 0)
    level = jnp.broadcast_to(level, (groups, BLK))
    my_filt = lax.dynamic_slice_in_dim(filt, h * groups, groups, 0)
    turned = my_filt.reshape(groups, NOFF, BLK)[:, :, ::-1].astype(F32)
    turned_shape = jax.ShapeDtypeStruct((groups, blocks * CPG, BLK), BF16)
    own, x_flip = call(
        own_kernel,
        "own",
        (turned_shape, jax.ShapeDtypeStruct((groups, BLK, blocks * CPG), BF16)),
        [SMEM] + [VMEM] * 4,
        [pltpu.VMEM(turned_shape.shape, BF16)],
    )(h[None], out_grad, swapped(out_grad), inputs, swapped(inputs))
    send, later = call(
        filt_grad_kernel,
        "filt_grad",
        (jax.ShapeDtypeStruct((NOFF, groups, LANES), F32), turned_shape),
        [SMEM] + [VMEM] * 5,
        [pltpu.VMEM((NOFF, groups, 8, BLK), F32)],
    )(h[None], level, x_flip, own, later_dy, swapped(later_dy))
    half = jax.ShapeDtypeStruct((blocks // 2, LANES, BLK), BF16)
    mine, theirs = call(
        in_grad_kernel,
        "in_grad",
        (half, half),
        [SMEM] + [VMEM] * 4,
    )(h[None], level, turned, own, later)
    dx = call(
        pack_kernel,
        "pack",
        jax.ShapeDtypeStruct((blocks // 2, 2 * LANES, BLK), BF16),
        [SMEM] + [VMEM] * 2,
    )(h[None], mine, lax.all_gather(theirs, "core"))

    got = lax.all_to_all(send, "z", 0, 0, tiled=True)
    wide = lax.all_to_all(dx, "grp", 0, 0, tiled=True)
    parts = lax.all_gather(jnp.sum(got, axis=0), ("xh", "core"))
    shift = (LANES - (2 * lax.axis_index("xh") + h) * QUART) % LANES
    scale = 1.0 / math.sqrt(rows * 2 * chips * CPG)
    return call(
        functools.partial(last_kernel, scale),
        "last",
        (
            jax.ShapeDtypeStruct((BLK, blocks * LANES), BF16),
            jax.ShapeDtypeStruct((2 * groups, QUART), F32),
        ),
        [SMEM] * 2 + [VMEM] * 2,
    )(h[None], shift[None], wide, parts)


def solution(mesh):
    seq, grp = mesh.shape["seq"], mesh.shape["grp"]
    split = Mesh(mesh.devices.reshape(seq // 4, 2, 2, grp), ("z", "xh", "core", "grp"))
    tokens = ("z", "xh", "core")
    return jax.shard_map(
        per_device,
        mesh=split,
        in_specs=(P(tokens, "grp"), P(tokens, "grp"), P("grp", None), P("grp", None)),
        out_specs=(P(tokens + ("grp",), None), P("grp", tokens)),
        check_vma=False,
    )
```

```python
import functools
import math

import jax
import jax.numpy as jnp
from jax import lax
from jax.experimental import pallas as pl
from jax.experimental.pallas import tpu as pltpu
from jax.sharding import Mesh
from jax.sharding import PartitionSpec as P

CPG = 16
BLK = 128
NOFF = 16
LANES = 128
QUART = 32
BF16 = jnp.bfloat16
F32 = jnp.float32
VMEM = pl.BlockSpec(memory_space=pltpu.VMEM)
SMEM = pl.BlockSpec(memory_space=pltpu.SMEM)
PARAMS = pltpu.CompilerParams(vmem_limit_bytes=24 << 20)


def aligned(start, size):
    return pl.ds(pl.multiple_of(start, size), size)


def transposed(block):
    return block.T.reshape(-1, CPG, BLK)


def turn(core, whole, gathered, out):
    per_core = whole.shape[0] // BLK
    mine = aligned(core * LANES, LANES) if whole.shape[1] > LANES else slice(None)
    for i in range(per_core):
        here = pl.ds(i * BLK, BLK)
        out[:, aligned((core * per_core + i) * CPG, CPG), :] = transposed(whole[here, mine])
        other = gathered[here, :] if len(gathered.shape) == 2 else gathered[1 - core, here, :]
        other = transposed(other)
        out[:, aligned(((1 - core) * per_core + i) * CPG, CPG), :] = other


def own_kernel(core, dy, dy_gathered, x, x_gathered, dy_out, x_out, x_t):
    row = lax.broadcasted_iota(jnp.int32, (BLK, BLK), 0)
    col = lax.broadcasted_iota(jnp.int32, (BLK, BLK), 1)
    flip = jnp.where(row + col == BLK - 1, 1.0, 0.0).astype(BF16)
    turn(core[0], dy, dy_gathered, dy_out)
    turn(core[0], x, x_gathered, x_t)
    for g in range(x_t.shape[0]):
        x_out[g] = lax.dot_general(
            flip, x_t[g], (((1,), (1,)), ((), ())), preferred_element_type=F32
        ).astype(BF16)


def window(own, later, g, k):
    if k == 0:
        return own[g]
    return jnp.concatenate([own[g, k * CPG :, :], later[g, : k * CPG, :]], axis=0)


def two_windows(own, later, g, k):
    return jnp.concatenate([window(own, later, g, k), window(own, later, g, k + 1)], axis=1)


def filt_grad_kernel(core, level, x_flip, own, dy, dy_gathered, send_ref, later, dh_ref):
    groups = own.shape[0]
    turn(core[0], dy, dy_gathered, later)
    row = lax.broadcasted_iota(jnp.int32, (BLK, BLK), 0)
    col = lax.broadcasted_iota(jnp.int32, (BLK, BLK), 1)
    within = row + col >= BLK - 1

    for g in range(groups):
        count = level[g : g + 1, :]

        def diagonals(k, now, after):
            after = 0.0 if after is None else jnp.where(k + 1 < count, after, 0.0)
            skew = pltpu.roll(jnp.where(within, now, after), 1, 1, stride=1, stride_axis=0)
            eight = jnp.sum(skew.reshape(BLK // 8, 8, BLK), axis=0)
            dh_ref[k, g] = jnp.where(k < count, eight, 0.0)

        last = None
        for two in range(0, NOFF, 2):
            product = jnp.dot(
                x_flip[g], two_windows(own, later, g, two), preferred_element_type=F32
            )
            now, after = product[:, :BLK], product[:, BLK:]
            if two:
                diagonals(two - 1, last, now)
            diagonals(two, now, after)
            last = after
        diagonals(NOFF - 1, last, None)

    sub = lax.broadcasted_iota(jnp.int32, (8, BLK), 0)
    for k in range(NOFF):
        send_ref[k] = column_sums([dh_ref[k, g] for g in range(groups)], sub)


def column_sums(parts, sub):
    for step in (4, 2, 1):
        low = sub % (2 * step) < step
        half = len(parts) // 2
        parts = [
            jnp.where(low, a, b) + pltpu.roll(jnp.where(low, b, a), step, 0)
            if step == 4
            else jnp.where(low, a + pltpu.roll(a, 8 - step, 0), b + pltpu.roll(b, step, 0))
            for a, b in zip(parts[:half], parts[half:])
        ]
    return parts[0]


def in_grad_kernel(core, level, turned_filt, own, later, mine, theirs):
    row = lax.broadcasted_iota(jnp.int32, (BLK, BLK), 0)
    col = lax.broadcasted_iota(jnp.int32, (BLK, BLK), 1)
    first = core[0] == 0

    def one_group(g, _):
        lags = turned_filt[g]
        count = level[pl.ds(g, 1), :]
        before = jnp.zeros((BLK, BLK), F32)
        tiles = []
        for k in range(NOFF):
            spread = jnp.broadcast_to(lags[k : k + 1], (BLK, BLK))
            here = pltpu.roll(spread, 1, 1, stride=1, stride_axis=0)
            tile = jnp.where(col > row, before, here)
            tiles.append(jnp.where(k < count, tile, 0.0).astype(BF16))
            before = here
        wide = jnp.concatenate([window(own, later, g, k) for k in range(NOFF)], axis=1)
        grad = jnp.dot(wide, jnp.concatenate(tiles, axis=0), preferred_element_type=F32)
        blocks = grad.reshape(2, -1, CPG, BLK).astype(BF16)
        mine[:, aligned(g * CPG, CPG), :] = jnp.where(first, blocks[0], blocks[1])
        theirs[:, aligned(g * CPG, CPG), :] = jnp.where(first, blocks[1], blocks[0])
        return 0

    lax.fori_loop(0, own.shape[0], one_group, 0, unroll=8)


def pack_kernel(core, mine, gathered, out):
    out[:, :LANES, :] = mine[...]
    out[:, LANES:, :] = gathered[1 - core[0]]


def last_kernel(scale, core, shift, got, parts, wide, narrow):
    cores = 2
    groups = parts.shape[1]
    first = core[0] == 0
    for r in range(got.shape[0]):
        mine = got[r, :LANES, :].T
        other = got[r, LANES:, :].T
        at = r * cores * LANES
        wide[:, at : at + LANES] = jnp.where(first, mine, other)
        wide[:, at + LANES : at + 2 * LANES] = jnp.where(first, other, mine)
    for h in range(cores):
        total = parts[h] + parts[cores + h]
        lags = pltpu.roll(total, shift[0], 1)[:, :QUART]
        narrow[h * groups : (h + 1) * groups, :] = lags * scale


def call(kernel, name, outs, in_specs, scratch=()):
    return pl.pallas_call(
        kernel,
        out_shape=outs,
        in_specs=in_specs,
        out_specs=jax.tree.map(lambda _: VMEM, outs),
        scratch_shapes=scratch,
        compiler_params=PARAMS,
        name=name,
    )


def per_device(inputs, out_grad, filt, band):
    rows, channels = inputs.shape
    groups = channels // CPG // 2
    blocks = 2 * rows // BLK
    chips = 2 * lax.axis_size("z")
    h = lax.axis_index("core")
    seq = ("z", "xh", "core")

    def swapped(whole):
        theirs = lax.dynamic_slice_in_dim(whole, (1 - h) * LANES, LANES, 1)
        return lax.all_gather(theirs, "core")

    def earlier_chip(block, swap):
        pairs = [(i, (i ^ swap) - 2) for i in range(2, 2 * chips)]
        return lax.ppermute(block, seq, pairs)

    later_same = earlier_chip(lax.dynamic_slice_in_dim(out_grad, h * LANES, LANES, 1), 0)
    later_other = earlier_chip(lax.dynamic_slice_in_dim(out_grad, (1 - h) * LANES, LANES, 1), 1)

    level = lax.dynamic_slice_in_dim(jnp.sum(band, axis=1, keepdims=True), h * groups, groups, 0)
    level = jnp.broadcast_to(level, (groups, BLK))
    my_filt = lax.dynamic_slice_in_dim(filt, h * groups, groups, 0)
    turned = my_filt.reshape(groups, NOFF, BLK)[:, :, ::-1].astype(F32)
    turned_shape = jax.ShapeDtypeStruct((groups, blocks * CPG, BLK), BF16)
    own, x_flip = call(
        own_kernel,
        "own",
        (turned_shape, jax.ShapeDtypeStruct((groups, BLK, blocks * CPG), BF16)),
        [SMEM] + [VMEM] * 4,
        [pltpu.VMEM(turned_shape.shape, BF16)],
    )(h[None], out_grad, swapped(out_grad), inputs, swapped(inputs))
    send, later = call(
        filt_grad_kernel,
        "filt_grad",
        (jax.ShapeDtypeStruct((NOFF, groups, LANES), F32), turned_shape),
        [SMEM] + [VMEM] * 5,
        [pltpu.VMEM((NOFF, groups, 8, BLK), F32)],
    )(h[None], level, x_flip, own, later_same, later_other)
    half = jax.ShapeDtypeStruct((blocks // 2, LANES, BLK), BF16)
    mine, theirs = call(
        in_grad_kernel,
        "in_grad",
        (half, half),
        [SMEM] + [VMEM] * 4,
    )(h[None], level, turned, own, later)
    dx = call(
        pack_kernel,
        "pack",
        jax.ShapeDtypeStruct((blocks // 2, 2 * LANES, BLK), BF16),
        [SMEM] + [VMEM] * 2,
    )(h[None], mine, lax.all_gather(theirs, "core"))

    got = lax.all_to_all(send, "z", 0, 0, tiled=True)
    wide = lax.all_to_all(dx, "grp", 0, 0, tiled=True)
    parts = lax.all_gather(jnp.sum(got, axis=0), ("xh", "core"))
    shift = (LANES - (2 * lax.axis_index("xh") + h) * QUART) % LANES
    scale = 1.0 / math.sqrt(rows * 2 * chips * CPG)
    return call(
        functools.partial(last_kernel, scale),
        "last",
        (
            jax.ShapeDtypeStruct((BLK, blocks * LANES), BF16),
            jax.ShapeDtypeStruct((2 * groups, QUART), F32),
        ),
        [SMEM] * 2 + [VMEM] * 2,
    )(h[None], shift[None], wide, parts)


def solution(mesh):
    seq, grp = mesh.shape["seq"], mesh.shape["grp"]
    split = Mesh(mesh.devices.reshape(seq // 4, 2, 2, grp), ("z", "xh", "core", "grp"))
    tokens = ("z", "xh", "core")
    return jax.shard_map(
        per_device,
        mesh=split,
        in_specs=(P(tokens, "grp"), P(tokens, "grp"), P("grp", None), P("grp", None)),
        out_specs=(P(tokens + ("grp",), None), P("grp", tokens)),
        check_vma=False,
    )
```

```python
import functools
import math

import jax
import jax.numpy as jnp
from jax import lax
from jax.experimental import pallas as pl
from jax.experimental.pallas import tpu as pltpu
from jax.sharding import Mesh
from jax.sharding import PartitionSpec as P

CPG = 16
BLK = 128
NOFF = 16
LANES = 128
QUART = 32
BF16 = jnp.bfloat16
F32 = jnp.float32
VMEM = pl.BlockSpec(memory_space=pltpu.VMEM)
ANY = pl.BlockSpec(memory_space=pl.ANY)
SMEM = pl.BlockSpec(memory_space=pltpu.SMEM)
PARAMS = pltpu.CompilerParams(vmem_limit_bytes=24 << 20)


def aligned(start, size):
    return pl.ds(pl.multiple_of(start, size), size)


def transposed(block):
    return block.T.reshape(-1, CPG, BLK)


def turn(core, whole, gathered, out):
    per_core = whole.shape[0] // BLK
    mine = aligned(core * LANES, LANES) if whole.shape[1] > LANES else slice(None)
    for i in range(per_core):
        here = pl.ds(i * BLK, BLK)
        out[:, aligned((core * per_core + i) * CPG, CPG), :] = transposed(whole[here, mine])
        other = gathered[here, :] if len(gathered.shape) == 2 else gathered[1 - core, here, :]
        other = transposed(other)
        out[:, aligned(((1 - core) * per_core + i) * CPG, CPG), :] = other


def own_kernel(core, dy, dy_gathered, x, x_gathered, dy_out, x_out, x_t):
    row = lax.broadcasted_iota(jnp.int32, (BLK, BLK), 0)
    col = lax.broadcasted_iota(jnp.int32, (BLK, BLK), 1)
    flip = jnp.where(row + col == BLK - 1, 1.0, 0.0).astype(BF16)
    turn(core[0], dy, dy_gathered, dy_out)
    turn(core[0], x, x_gathered, x_t)
    for g in range(x_t.shape[0]):
        x_out[g] = lax.dot_general(
            flip, x_t[g], (((1,), (1,)), ((), ())), preferred_element_type=F32
        ).astype(BF16)


def window(own, later, g, k):
    if k == 0:
        return own[g]
    return jnp.concatenate([own[g, k * CPG :, :], later[g, : k * CPG, :]], axis=0)


def two_windows(own, later, g, k):
    return jnp.concatenate([window(own, later, g, k), window(own, later, g, k + 1)], axis=1)


def filt_grad_kernel(core, level, x_flip, own, dy, dy_gathered, send_ref, later, dh_ref):
    groups = own.shape[0]
    turn(core[0], dy, dy_gathered, later)
    row = lax.broadcasted_iota(jnp.int32, (BLK, BLK), 0)
    col = lax.broadcasted_iota(jnp.int32, (BLK, BLK), 1)
    within = row + col >= BLK - 1

    for g in range(groups):
        count = level[g : g + 1, :]

        def diagonals(k, now, after):
            after = 0.0 if after is None else jnp.where(k + 1 < count, after, 0.0)
            skew = pltpu.roll(jnp.where(within, now, after), 1, 1, stride=1, stride_axis=0)
            eight = jnp.sum(skew.reshape(BLK // 8, 8, BLK), axis=0)
            dh_ref[k, g] = jnp.where(k < count, eight, 0.0)

        last = None
        for two in range(0, NOFF, 2):
            product = jnp.dot(
                x_flip[g], two_windows(own, later, g, two), preferred_element_type=F32
            )
            now, after = product[:, :BLK], product[:, BLK:]
            if two:
                diagonals(two - 1, last, now)
            diagonals(two, now, after)
            last = after
        diagonals(NOFF - 1, last, None)

    sub = lax.broadcasted_iota(jnp.int32, (8, BLK), 0)
    for k in range(NOFF):
        send_ref[k] = column_sums([dh_ref[k, g] for g in range(groups)], sub)


def column_sums(parts, sub):
    for step in (4, 2, 1):
        low = sub % (2 * step) < step
        half = len(parts) // 2
        parts = [
            jnp.where(low, a, b) + pltpu.roll(jnp.where(low, b, a), step, 0)
            if step == 4
            else jnp.where(low, a + pltpu.roll(a, 8 - step, 0), b + pltpu.roll(b, step, 0))
            for a, b in zip(parts[:half], parts[half:])
        ]
    return parts[0]


def in_grad_kernel(core, level, turned_filt, own, later, mine, theirs):
    row = lax.broadcasted_iota(jnp.int32, (BLK, BLK), 0)
    col = lax.broadcasted_iota(jnp.int32, (BLK, BLK), 1)
    first = core[0] == 0

    def one_group(g, _):
        lags = turned_filt[g]
        count = level[pl.ds(g, 1), :]
        before = jnp.zeros((BLK, BLK), F32)
        tiles = []
        for k in range(NOFF):
            spread = jnp.broadcast_to(lags[k : k + 1], (BLK, BLK))
            here = pltpu.roll(spread, 1, 1, stride=1, stride_axis=0)
            tile = jnp.where(col > row, before, here)
            tiles.append(jnp.where(k < count, tile, 0.0).astype(BF16))
            before = here
        wide = jnp.concatenate([window(own, later, g, k) for k in range(NOFF)], axis=1)
        grad = jnp.dot(wide, jnp.concatenate(tiles, axis=0), preferred_element_type=F32)
        blocks = grad.reshape(2, -1, CPG, BLK).astype(BF16)
        mine[:, aligned(g * CPG, CPG), :] = jnp.where(first, blocks[0], blocks[1])
        theirs[:, aligned(g * CPG, CPG), :] = jnp.where(first, blocks[1], blocks[0])
        return 0

    lax.fori_loop(0, own.shape[0], one_group, 0, unroll=8)


def pack_kernel(core, mine, gathered, out, sems):
    first = pltpu.make_async_copy(mine, out.at[:, :LANES, :], sems.at[0])
    second = pltpu.make_async_copy(gathered.at[1 - core[0]], out.at[:, LANES:, :], sems.at[1])
    first.start()
    second.start()
    first.wait()
    second.wait()


def last_kernel(scale, core, shift, got, parts, wide, narrow):
    cores = 2
    groups = parts.shape[1]
    first = core[0] == 0
    for r in range(got.shape[0]):
        mine = got[r, :LANES, :].T
        other = got[r, LANES:, :].T
        at = r * cores * LANES
        wide[:, at : at + LANES] = jnp.where(first, mine, other)
        wide[:, at + LANES : at + 2 * LANES] = jnp.where(first, other, mine)
    for h in range(cores):
        total = parts[h] + parts[cores + h]
        lags = pltpu.roll(total, shift[0], 1)[:, :QUART]
        narrow[h * groups : (h + 1) * groups, :] = lags * scale


def call(kernel, name, outs, in_specs, scratch=(), space=VMEM):
    return pl.pallas_call(
        kernel,
        out_shape=outs,
        in_specs=in_specs,
        out_specs=jax.tree.map(lambda _: space, outs),
        scratch_shapes=scratch,
        compiler_params=PARAMS,
        name=name,
    )


def per_device(inputs, out_grad, filt, band):
    rows, channels = inputs.shape
    groups = channels // CPG // 2
    blocks = 2 * rows // BLK
    chips = 2 * lax.axis_size("z")
    h = lax.axis_index("core")
    seq = ("z", "xh", "core")

    def swapped(whole):
        theirs = lax.dynamic_slice_in_dim(whole, (1 - h) * LANES, LANES, 1)
        return lax.all_gather(theirs, "core")

    def earlier_chip(block, swap):
        pairs = [(i, (i ^ swap) - 2) for i in range(2, 2 * chips)]
        return lax.ppermute(block, seq, pairs)

    later_same = earlier_chip(lax.dynamic_slice_in_dim(out_grad, h * LANES, LANES, 1), 0)
    later_other = earlier_chip(lax.dynamic_slice_in_dim(out_grad, (1 - h) * LANES, LANES, 1), 1)

    level = lax.dynamic_slice_in_dim(jnp.sum(band, axis=1, keepdims=True), h * groups, groups, 0)
    level = jnp.broadcast_to(level, (groups, BLK))
    my_filt = lax.dynamic_slice_in_dim(filt, h * groups, groups, 0)
    turned = my_filt.reshape(groups, NOFF, BLK)[:, :, ::-1].astype(F32)
    turned_shape = jax.ShapeDtypeStruct((groups, blocks * CPG, BLK), BF16)
    own, x_flip = call(
        own_kernel,
        "own",
        (turned_shape, jax.ShapeDtypeStruct((groups, BLK, blocks * CPG), BF16)),
        [SMEM] + [VMEM] * 4,
        [pltpu.VMEM(turned_shape.shape, BF16)],
    )(h[None], out_grad, swapped(out_grad), inputs, swapped(inputs))
    send, later = call(
        filt_grad_kernel,
        "filt_grad",
        (jax.ShapeDtypeStruct((NOFF, groups, LANES), F32), turned_shape),
        [SMEM] + [VMEM] * 5,
        [pltpu.VMEM((NOFF, groups, 8, BLK), F32)],
    )(h[None], level, x_flip, own, later_same, later_other)
    half = jax.ShapeDtypeStruct((blocks // 2, LANES, BLK), BF16)
    mine, theirs = call(
        in_grad_kernel,
        "in_grad",
        (half, half),
        [SMEM] + [VMEM] * 4,
    )(h[None], level, turned, own, later)
    dx = call(
        pack_kernel,
        "pack",
        jax.ShapeDtypeStruct((blocks // 2, 2 * LANES, BLK), BF16),
        [SMEM] + [ANY] * 2,
        [pltpu.SemaphoreType.DMA((2,))],
        ANY,
    )(h[None], mine, lax.all_gather(theirs, "core"))

    got = lax.all_to_all(send, "z", 0, 0, tiled=True)
    wide = lax.all_to_all(dx, "grp", 0, 0, tiled=True)
    parts = lax.all_gather(jnp.sum(got, axis=0), ("xh", "core"))
    shift = (LANES - (2 * lax.axis_index("xh") + h) * QUART) % LANES
    scale = 1.0 / math.sqrt(rows * 2 * chips * CPG)
    return call(
        functools.partial(last_kernel, scale),
        "last",
        (
            jax.ShapeDtypeStruct((BLK, blocks * LANES), BF16),
            jax.ShapeDtypeStruct((2 * groups, QUART), F32),
        ),
        [SMEM] * 2 + [VMEM] * 2,
    )(h[None], shift[None], wide, parts)


def solution(mesh):
    seq, grp = mesh.shape["seq"], mesh.shape["grp"]
    split = Mesh(mesh.devices.reshape(seq // 4, 2, 2, grp), ("z", "xh", "core", "grp"))
    tokens = ("z", "xh", "core")
    return jax.shard_map(
        per_device,
        mesh=split,
        in_specs=(P(tokens, "grp"), P(tokens, "grp"), P("grp", None), P("grp", None)),
        out_specs=(P(tokens + ("grp",), None), P("grp", tokens)),
        check_vma=False,
    )
```

```python
import functools
import math

import jax
import jax.numpy as jnp
from jax import lax
from jax.experimental import pallas as pl
from jax.experimental.pallas import tpu as pltpu
from jax.sharding import Mesh
from jax.sharding import PartitionSpec as P

CPG = 16
BLK = 128
NOFF = 16
LANES = 128
QUART = 32
BF16 = jnp.bfloat16
F32 = jnp.float32
VMEM = pl.BlockSpec(memory_space=pltpu.VMEM)
SMEM = pl.BlockSpec(memory_space=pltpu.SMEM)
PARAMS = pltpu.CompilerParams(vmem_limit_bytes=24 << 20)


def aligned(start, size):
    return pl.ds(pl.multiple_of(start, size), size)


def transposed(block):
    return block.T.reshape(-1, CPG, BLK)


def turn(core, whole, gathered, out):
    per_core = whole.shape[0] // BLK
    mine = aligned(core * LANES, LANES) if whole.shape[1] > LANES else slice(None)
    for i in range(per_core):
        here = pl.ds(i * BLK, BLK)
        out[:, aligned((core * per_core + i) * CPG, CPG), :] = transposed(whole[here, mine])
        other = gathered[here, :] if len(gathered.shape) == 2 else gathered[1 - core, here, :]
        other = transposed(other)
        out[:, aligned(((1 - core) * per_core + i) * CPG, CPG), :] = other


def own_kernel(core, dy, dy_gathered, x, x_gathered, dy_out, x_out, x_t):
    row = lax.broadcasted_iota(jnp.int32, (BLK, BLK), 0)
    col = lax.broadcasted_iota(jnp.int32, (BLK, BLK), 1)
    flip = jnp.where(row + col == BLK - 1, 1.0, 0.0).astype(BF16)
    turn(core[0], dy, dy_gathered, dy_out)
    turn(core[0], x, x_gathered, x_t)
    for g in range(x_t.shape[0]):
        x_out[g] = lax.dot_general(
            flip, x_t[g], (((1,), (1,)), ((), ())), preferred_element_type=F32
        ).astype(BF16)


def window(own, later, g, k):
    if k == 0:
        return own[g]
    return jnp.concatenate([own[g, k * CPG :, :], later[g, : k * CPG, :]], axis=0)


def two_windows(own, later, g, k):
    return jnp.concatenate([window(own, later, g, k), window(own, later, g, k + 1)], axis=1)


def filt_grad_kernel(core, level, x_flip, own, dy, dy_gathered, send_ref, later, dh_ref):
    groups = own.shape[0]
    turn(core[0], dy, dy_gathered, later)
    row = lax.broadcasted_iota(jnp.int32, (BLK, BLK), 0)
    col = lax.broadcasted_iota(jnp.int32, (BLK, BLK), 1)
    within = row + col >= BLK - 1

    for g in range(groups):
        count = level[g : g + 1, :]

        def diagonals(k, now, after):
            after = 0.0 if after is None else jnp.where(k + 1 < count, after, 0.0)
            skew = pltpu.roll(jnp.where(within, now, after), 1, 1, stride=1, stride_axis=0)
            eight = jnp.sum(skew.reshape(BLK // 8, 8, BLK), axis=0)
            dh_ref[k, g] = jnp.where(k < count, eight, 0.0)

        last = None
        for two in range(0, NOFF, 2):
            product = jnp.dot(
                x_flip[g], two_windows(own, later, g, two), preferred_element_type=F32
            )
            now, after = product[:, :BLK], product[:, BLK:]
            if two:
                diagonals(two - 1, last, now)
            diagonals(two, now, after)
            last = after
        diagonals(NOFF - 1, last, None)

    sub = lax.broadcasted_iota(jnp.int32, (8, BLK), 0)
    for k in range(NOFF):
        send_ref[k] = column_sums([dh_ref[k, g] for g in range(groups)], sub)


def column_sums(parts, sub):
    for step in (4, 2, 1):
        low = sub % (2 * step) < step
        half = len(parts) // 2
        parts = [
            jnp.where(low, a, b) + pltpu.roll(jnp.where(low, b, a), step, 0)
            if step == 4
            else jnp.where(low, a + pltpu.roll(a, 8 - step, 0), b + pltpu.roll(b, step, 0))
            for a, b in zip(parts[:half], parts[half:])
        ]
    return parts[0]


def in_grad_kernel(core, level, turned_filt, own, later, mine, theirs):
    row = lax.broadcasted_iota(jnp.int32, (BLK, BLK), 0)
    col = lax.broadcasted_iota(jnp.int32, (BLK, BLK), 1)
    first = core[0] == 0

    def one_group(g, _):
        lags = turned_filt[g]
        count = level[pl.ds(g, 1), :]
        before = jnp.zeros((BLK, BLK), F32)
        tiles = []
        for k in range(NOFF):
            spread = jnp.broadcast_to(lags[k : k + 1], (BLK, BLK))
            here = pltpu.roll(spread, 1, 1, stride=1, stride_axis=0)
            tile = jnp.where(col > row, before, here)
            tiles.append(jnp.where(k < count, tile, 0.0).astype(BF16))
            before = here
        wide = jnp.concatenate([window(own, later, g, k) for k in range(NOFF)], axis=1)
        grad = jnp.dot(wide, jnp.concatenate(tiles, axis=0), preferred_element_type=F32)
        blocks = grad.reshape(2, -1, CPG, BLK).astype(BF16)
        mine[:, aligned(g * CPG, CPG), :] = jnp.where(first, blocks[0], blocks[1])
        theirs[:, aligned(g * CPG, CPG), :] = jnp.where(first, blocks[1], blocks[0])
        return 0

    lax.fori_loop(0, own.shape[0], one_group, 0, unroll=8)


def pack_kernel(core, mine, gathered, out):
    out[:, :LANES, :] = mine[...]
    out[:, LANES:, :] = gathered[1 - core[0]]


def last_kernel(scale, core, shift, got, parts, wide, narrow):
    cores = 2
    groups = parts.shape[1]
    first = core[0] == 0
    for r in range(got.shape[0]):
        mine = got[r, :LANES, :].T
        other = got[r, LANES:, :].T
        at = r * cores * LANES
        wide[:, at : at + LANES] = jnp.where(first, mine, other)
        wide[:, at + LANES : at + 2 * LANES] = jnp.where(first, other, mine)
    for h in range(cores):
        total = parts[h] + parts[cores + h]
        lags = pltpu.roll(total, shift[0], 1)[:, :QUART]
        narrow[h * groups : (h + 1) * groups, :] = lags * scale


def call(kernel, name, outs, in_specs, scratch=()):
    return pl.pallas_call(
        kernel,
        out_shape=outs,
        in_specs=in_specs,
        out_specs=jax.tree.map(lambda _: VMEM, outs),
        scratch_shapes=scratch,
        compiler_params=PARAMS,
        name=name,
    )


def per_device(inputs, out_grad, filt, band):
    rows, channels = inputs.shape
    groups = channels // CPG // 2
    blocks = 2 * rows // BLK
    chips = 2 * lax.axis_size("z")
    h = lax.axis_index("core")
    seq = ("z", "xh", "core")

    def swapped(whole):
        theirs = lax.dynamic_slice_in_dim(whole, (1 - h) * LANES, LANES, 1)
        return lax.all_gather(theirs, "core")

    def earlier_chip(block, swap):
        pairs = [(i, (i ^ swap) - 2) for i in range(2, 2 * chips)]
        return lax.ppermute(block, seq, pairs)

    dy_mine = lax.dynamic_slice_in_dim(out_grad, h * LANES, LANES, 1)
    later_same = earlier_chip(dy_mine, 0)
    later_other = earlier_chip(lax.dynamic_slice_in_dim(out_grad, (1 - h) * LANES, LANES, 1), 1)

    level = lax.dynamic_slice_in_dim(jnp.sum(band, axis=1, keepdims=True), h * groups, groups, 0)
    level = jnp.broadcast_to(level, (groups, BLK))
    my_filt = lax.dynamic_slice_in_dim(filt, h * groups, groups, 0)
    turned = my_filt.reshape(groups, NOFF, BLK)[:, :, ::-1].astype(F32)
    turned_shape = jax.ShapeDtypeStruct((groups, blocks * CPG, BLK), BF16)
    own, x_flip = call(
        own_kernel,
        "own",
        (turned_shape, jax.ShapeDtypeStruct((groups, BLK, blocks * CPG), BF16)),
        [SMEM] + [VMEM] * 4,
        [pltpu.VMEM(turned_shape.shape, BF16)],
    )(h[None], dy_mine, swapped(out_grad), inputs, swapped(inputs))
    send, later = call(
        filt_grad_kernel,
        "filt_grad",
        (jax.ShapeDtypeStruct((NOFF, groups, LANES), F32), turned_shape),
        [SMEM] + [VMEM] * 5,
        [pltpu.VMEM((NOFF, groups, 8, BLK), F32)],
    )(h[None], level, x_flip, own, later_same, later_other)
    half = jax.ShapeDtypeStruct((blocks // 2, LANES, BLK), BF16)
    mine, theirs = call(
        in_grad_kernel,
        "in_grad",
        (half, half),
        [SMEM] + [VMEM] * 4,
    )(h[None], level, turned, own, later)
    dx = call(
        pack_kernel,
        "pack",
        jax.ShapeDtypeStruct((blocks // 2, 2 * LANES, BLK), BF16),
        [SMEM] + [VMEM] * 2,
    )(h[None], mine, lax.all_gather(theirs, "core"))

    got = lax.all_to_all(send, "z", 0, 0, tiled=True)
    wide = lax.all_to_all(dx, "grp", 0, 0, tiled=True)
    parts = lax.all_gather(jnp.sum(got, axis=0), ("xh", "core"))
    shift = (LANES - (2 * lax.axis_index("xh") + h) * QUART) % LANES
    scale = 1.0 / math.sqrt(rows * 2 * chips * CPG)
    return call(
        functools.partial(last_kernel, scale),
        "last",
        (
            jax.ShapeDtypeStruct((BLK, blocks * LANES), BF16),
            jax.ShapeDtypeStruct((2 * groups, QUART), F32),
        ),
        [SMEM] * 2 + [VMEM] * 2,
    )(h[None], shift[None], wide, parts)


def solution(mesh):
    seq, grp = mesh.shape["seq"], mesh.shape["grp"]
    split = Mesh(mesh.devices.reshape(seq // 4, 2, 2, grp), ("z", "xh", "core", "grp"))
    tokens = ("z", "xh", "core")
    return jax.shard_map(
        per_device,
        mesh=split,
        in_specs=(P(tokens, "grp"), P(tokens, "grp"), P("grp", None), P("grp", None)),
        out_specs=(P(tokens + ("grp",), None), P("grp", tokens)),
        check_vma=False,
    )
```
